512 devices in a mesh: rows: 64 (over z, x, core), cols: 8 (over y).
Axes of the slice: x: 4, y: 8, z: 8, core: 2. Of those that a mesh axis runs over, the one named last changes fastest.
Arguments:
- panel: bfloat16 [131072, 8192], P('rows', 'cols'), may hold values from -100 to 100
- omega: bfloat16 [8192, 128], P('cols'), may hold values from -0.0625 to 0.0625
- order: int32 [128], replicated, may hold values from 0 to 127, each once
Outputs:
- basis: bfloat16 [131072, 128], P('rows')
- coefficients: float32 [8192, 128], P(('cols', 'rows'))
The draws below stay inside these ranges and needn't reach their ends.
Inputs may be any that keep to these rules, and one draw needn't show every extreme that they name: order holds each of 0 to 127 once.
All inputs are finite; a program needn't handle non-finite values.
Results may differ from the reference program's by a relative error of at most 0.0016.
Values may be sent and summed in bfloat16 or wider, within the bound.
A program may use at most 128 MiB of HBM per device.

```python
import math
import jax
import jax.numpy as jnp
from jax import lax

SKETCH = 128
PANEL_ROWS = 131072
SNAPSHOTS = 8192


mode_count = 24


mode_decay = 0.8


noise_level = 0.3


overall = 0.05


def draw_panel(key, part):
    key = jax.random.fold_in(key, 7)
    keys = jax.random.split(key, 7)
    key_base, key_rows, key_cols, key_modes, key_angles, key_centers, key_phases = keys
    position = jnp.arange(PANEL_ROWS, dtype=jnp.float32)[:, None] / (PANEL_ROWS - 1)
    row_scale = jnp.exp(jax.random.uniform(key_rows, (PANEL_ROWS, 1), jnp.float32, 0.0, math.log(10.0)))
    rise = 1.0 + 2.0 * position
    angles = jax.random.uniform(key_angles, (1, SNAPSHOTS), jnp.float32, -math.pi, math.pi)
    centers = jax.random.uniform(key_centers, (mode_count,), jnp.float32, 0.0, 1.0)
    phases = jax.random.uniform(key_phases, (mode_count,), jnp.float32, -math.pi, math.pi)
    modes = jax.random.truncated_normal(key_modes, -3.0, 3.0, (PANEL_ROWS, mode_count), jnp.float32)
    base = jax.random.truncated_normal(key_base, -6.0, 6.0, (PANEL_ROWS, SNAPSHOTS), jnp.float32)
    signal = jnp.zeros((PANEL_ROWS, SNAPSHOTS), jnp.float32)
    for index in range(mode_count):
        envelope = 0.25 + 1.5 * jnp.exp(-jnp.square((position - centers[index]) / 0.12))
        shape_row = mode_decay ** index * modes[:, index:index + 1] * envelope
        shape_col = jnp.cos((index + 1) * angles + phases[index])
        signal = signal + shape_row * shape_col
    return (overall * (signal + noise_level * base) * row_scale * rise).astype(jnp.bfloat16)


def steps_of(key, shape, shards, least, top_value):
    def one(axis_at, parts):
        draws = jax.random.uniform(jax.random.fold_in(jax.random.fold_in(key, 6), axis_at), (parts,), jnp.float32, least / len(shards), top_value / len(shards))
        return jnp.repeat(jnp.exp(draws), shape[axis_at] // parts).reshape((-1,) + (1,) * (len(shape) - axis_at - 1))

    level = one(*shards[0])
    for cut in shards[1:]:
        level = level * one(*cut)
    return level


def noise(rng, extent, width, most, pieces=(), kind=jnp.bfloat16):
    result = width * jax.random.normal(rng, extent, jnp.float32)
    if pieces:
        result = result * steps_of(rng, extent, pieces, -0.22, 0.18)
    return jnp.clip(result, -most, most).astype(kind)


def setup_inputs(seed: int = 0) -> dict:
    key_list = jax.random.split(jax.random.key(seed), 4)
    return {
        "panel": draw_panel(jax.random.fold_in(key_list[3], 71), 0),
        "omega": noise(key_list[1], (SNAPSHOTS, SKETCH), SNAPSHOTS ** -0.5, 0.0625, ((0, 8),)),
        "order": jax.random.permutation(key_list[2], SKETCH).astype(jnp.int32),
    }


def reference(panel, omega, order):
    test = omega[:, order]
    sketch_y = jnp.dot(panel.astype(jnp.float32), test.astype(jnp.float32), preferred_element_type=jnp.float32)
    gram = jnp.dot(sketch_y.T, sketch_y, precision=lax.Precision.HIGHEST) / PANEL_ROWS
    lower = jnp.linalg.cholesky(gram)
    basis = lax.linalg.triangular_solve(lower, sketch_y, left_side=False, lower=True, transpose_a=True).astype(jnp.bfloat16)
    coefficients = lax.dot_general(panel.astype(jnp.float32), basis.astype(jnp.float32), (((0,), (0,)), ((), ())), preferred_element_type=jnp.float32)
    return (basis, coefficients / jnp.sqrt(jnp.float32(PANEL_ROWS)))
```

```python
import functools

import jax
import jax.numpy as jnp
from jax import lax
from jax.experimental import pallas as pl
from jax.experimental.pallas import tpu as pltpu
from jax.sharding import PartitionSpec as P

F32 = jnp.float32
BF16 = jnp.bfloat16
MESH = pl.DeviceIdType.MESH
K = 128
NY = 8
NZ = 8
NG = 8
HIGH = lax.Precision.HIGHEST

RIGHTWARD = ((4, 0), (3, 1), (3, 0), (2, 1), (2, 0), (1, 1), (1, 0))
LEFTWARD = ((4, 1), (5, 0), (5, 1), (6, 0), (6, 1), (7, 0), (7, 1))
CHUNKS = (4, 3, 5, 2, 6, 1, 7, 0)


def wide(v):
    return jnp.broadcast_to(v, (8, K))


def factor_block(rows, done, k):
    lane = lax.broadcasted_iota(jnp.int32, (8, K), 1)
    sub = lax.broadcasted_iota(jnp.int32, (8, K), 0)
    b0 = k // 8
    here = rows[b0]
    inside = (lane >= k) & (lane < k + 8)
    cols = [wide(here[:, k + j : k + j + 1]) for j in range(8)]
    s = {(i, j): wide(cols[j][i : i + 1, :]) for i in range(8) for j in range(i + 1)}
    mod = jnp.where(inside, jnp.where(lane - k == sub, 1.0, 0.0), here)
    a = [wide(mod[i : i + 1, :]) for i in range(8)]
    r, low, b = [], {}, []
    for j in range(8):
        r.append(pltpu.reciprocal(s[j, j], approx=False))
        for i in range(j + 1, 8):
            low[i, j] = s[i, j] * r[j]
        for i in range(j + 1, 8):
            for m in range(j + 1, i + 1):
                s[i, m] = s[i, m] - low[i, j] * s[m, j]
    for j in range(8):
        t = a[j]
        for m in range(j):
            t = t - low[j, m] * b[m]
        b.append(t)
    al = [None] * 8
    for j in reversed(range(8)):
        t = b[j] * r[j]
        for m in range(j + 1, 8):
            t = t - low[m, j] * al[m]
        al[j] = t
    out = jnp.zeros((8, K), F32)
    for j in range(8):
        out = jnp.where(sub == j, b[j] * lax.rsqrt(s[j, j]), out)
    done.append(jnp.where(lane <= sub + k, out, 0.0))
    for i in range(b0 + 1, 16):
        acc = jnp.where(inside, 0.0, rows[i])
        for j in range(8):
            acc = acc - wide(rows[i][:, k + j : k + j + 1]) * al[j]
        rows[i] = acc


def kernel(
    total_rows, panel_hbm, omega_hbm, order_ref, basis_hbm, coef_hbm,
    panel_v, omega_v, py, rr, rl, gram_v, a1, a2, a3, gram_f, yh, zt, zr, c1, w1, c2, w2, c3, basis_v, coef_v,
    panel_sem, omega_sem, out_sem, rs_send, rs_recv, g_send, g_recv, ag_send, ag_recv, z_send, z_recv,
):
    rows_at = lax.axis_index("rows")
    y = lax.axis_index("cols")
    z = rows_at // NG
    g = lax.rem(rows_at, NG)
    x = g // 2
    core = lax.rem(g, 2)
    nx = NG // 2

    def at_y(o):
        return (rows_at, lax.rem(y + o, NY))

    def at_z(o):
        return (lax.rem(z + o, NZ) * NG + g, y)

    def at_g(o):
        return (z * NG + lax.rem(g + o, NG), y)

    def send(src, dst, send_sem, recv_sem, device):
        c = pltpu.make_async_remote_copy(
            src_ref=src, dst_ref=dst, send_sem=send_sem, recv_sem=recv_sem, device_id=device, device_id_type=MESH
        )
        c.start()
        sent.append(c)
        return c

    sent = []
    ch = panel_v.shape[1]
    half = ch // 2

    loads = {}
    om = pltpu.make_async_copy(omega_hbm, omega_v, omega_sem)
    om.start()
    for j in CHUNKS:
        loads[j] = pltpu.make_async_copy(
            panel_hbm.at[pl.ds(pl.multiple_of(lax.rem(y + j, NY) * ch, ch), ch), :], panel_v.at[j], panel_sem.at[j]
        )
        loads[j].start()

    barrier = pltpu.get_barrier_semaphore()
    partners = [at_y(o) for o in range(1, NY)] + [at_z(o) for o in range(1, NZ)] + [at_g(o) for o in range(1, NG)]
    for device in partners:
        pl.semaphore_signal(barrier, inc=1, device_id=device, device_id_type=MESH)

    om.wait()
    picker = (order_ref[...] == lax.broadcasted_iota(jnp.int32, (K, K), 0)).astype(BF16)
    omega_v[...] = jnp.dot(omega_v[...], picker, preferred_element_type=F32).astype(BF16)

    def sketch(j):
        loads[j].wait()
        py[j] = jnp.dot(panel_v[j], omega_v[...], preferred_element_type=F32).reshape(2, half, K)

    right, left = at_y(1), at_y(NY - 1)
    copies_r, copies_l = [], []

    def rs_right(i):
        j, h = RIGHTWARD[i]
        if i >= 2:
            copies_r[i - 2].wait_recv()
            py[j, h] = py[j, h] + rr[i - 2]
        copies_r.append(send(py.at[j, h], rr.at[i], rs_send.at[0, i], rs_recv.at[0, i], right))

    def rs_left(i):
        j, h = LEFTWARD[i]
        if i >= 2:
            copies_l[i - 2].wait_recv()
            py[j, h] = py[j, h] + rl[i - 2]
        copies_l.append(send(py.at[j, h], rl.at[i], rs_send.at[1, i], rs_recv.at[1, i], left))

    sketch(4)
    pl.semaphore_wait(barrier, len(partners))
    rs_right(0)
    rs_left(0)
    sketch(3)
    rs_right(1)
    sketch(5)
    rs_left(1)
    for j in (2, 6, 1, 7, 0):
        sketch(j)
    for i in range(2, 7):
        rs_right(i)
        rs_left(i)
    copies_r[5].wait_recv()
    copies_l[5].wait_recv()
    part_b = py[0, 1] + rr[5]
    part_a = py[0, 0] + rl[5]
    copies_r[6].wait_recv()
    copies_l[6].wait_recv()
    share = jnp.concatenate([part_a + rr[6], part_b + rl[6]], axis=0)

    gram_v[...] = (
        lax.dot_general(share, share, (((0,), (0,)), ((), ())), precision=HIGH, preferred_element_type=F32) / total_rows
    ).reshape(NG, K // NG, K)
    st1 = [
        send(gram_v.at[lax.rem(g + o, NG)], a1.at[o], g_send.at[0, o], g_recv.at[0, o], at_g(o)) for o in range(1, NG)
    ]
    share_hi = share.astype(BF16)
    yh[0, 0] = share_hi.reshape(2, half, K)
    yh[1, 0] = (share - share_hi.astype(F32)).astype(BF16).reshape(2, half, K)

    hops = {}

    def gather_hop(kind, s):
        for way, device in ((0, right), (1, left)):
            src = (NY - s) % NY if way == 0 else s
            dst = NY - 1 - s if way == 0 else s + 1
            for h in (0, 1) if s < 3 else (way,):
                if s > 0:
                    hops[kind, s - 1, way, h].wait_recv()
                i = 2 * s + h
                hops[kind, s, way, h] = send(
                    yh.at[kind, src, h], yh.at[kind, dst, h], ag_send.at[kind, way, i], ag_recv.at[kind, way, i], device
                )

    def finish_gather(kind):
        hops[kind, 2, 0, 1].wait_recv()
        hops[kind, 2, 1, 0].wait_recv()
        hops[kind, 3, 0, 0].wait_recv()
        hops[kind, 3, 1, 1].wait_recv()

    def project(j, first=False):
        term = lax.dot_general(
            yh[0, j].reshape(ch, K), panel_v[j], (((0,), (0,)), ((), ())), preferred_element_type=F32
        )
        zt[...] = term if first else zt[...] + term

    gather_hop(0, 0)
    project(0, True)

    for c in st1:
        c.wait_recv()
    part = gram_v[g]
    for o in range(1, NG):
        part = part + a1[o]
    a2[y] = part
    st2 = [send(a2.at[y], a2.at[y], g_send.at[1, o], g_recv.at[1, o], at_y(o)) for o in range(1, NY)]

    gather_hop(0, 1)
    project(7)
    project(1)

    for c in st2:
        c.wait_recv()
    part = a2[0]
    for o in range(1, NY):
        part = part + a2[o]
    a3[z] = part
    st3 = [send(a3.at[z], a3.at[z], g_send.at[2, o], g_recv.at[2, o], at_z(o)) for o in range(1, NZ)]

    gather_hop(0, 2)
    project(6)
    project(2)

    for c in st3:
        c.wait_recv()
    part = a3[0]
    for o in range(1, NZ):
        part = part + a3[o]
    gram_f[g] = part
    st4 = [send(gram_f.at[g], gram_f.at[g], g_send.at[3, o], g_recv.at[3, o], at_g(o)) for o in range(1, NG)]

    gather_hop(0, 3)
    gather_hop(1, 0)
    finish_gather(0)
    project(5)
    project(3)
    project(4)

    per_z = NG * 16
    for b in range(NZ):
        block = zt[:, b * per_z : (b + 1) * per_z].T.reshape(nx, 2, 16, K)
        for h in range(2):
            for i in range(nx):
                zr[h, i, b] = block[i, h]
    other = (z * NG + g + 1 - 2 * core, y)
    zc = send(zr.at[1 - core], c1, z_send.at[0], z_recv.at[0], other)
    gather_hop(1, 1)

    for c in st4:
        c.wait_recv()
    matrix = gram_f[...].reshape(K, K)
    blocks = [matrix[8 * i : 8 * i + 8, :] for i in range(16)]
    done = []
    for k in range(0, 40, 8):
        factor_block(blocks, done, k)

    zc.wait_recv()
    w1[...] = zr[core] + c1[...]
    zx = [
        send(
            w1.at[lax.rem(x + o, nx)], c2.at[o], z_send.at[o], z_recv.at[o],
            (z * NG + lax.rem(x + o, nx) * 2 + core, y),
        )
        for o in range(1, nx)
    ]
    gather_hop(1, 2)
    for k in range(40, 88, 8):
        factor_block(blocks, done, k)
    total = w1[x]
    for o in range(1, nx):
        zx[o - 1].wait_recv()
        total = total + c2[o]
    w2[...] = total
    zz = [
        send(w2.at[lax.rem(z + o, NZ)], c3.at[o], z_send.at[3 + o], z_recv.at[3 + o], at_z(o)) for o in range(1, NZ)
    ]
    gather_hop(1, 3)
    for k in range(88, 128, 8):
        factor_block(blocks, done, k)

    inverse_t = jnp.concatenate(done, axis=0).T
    inv_hi = inverse_t.astype(BF16)
    inv_lo = (inverse_t - inv_hi.astype(F32)).astype(BF16)
    both = jnp.concatenate([inv_hi, inv_lo], axis=1)
    both = jnp.concatenate([both, both], axis=0)
    finish_gather(1)
    outs = []
    for j in range(NY):
        pair = jnp.concatenate([yh[0, j].reshape(ch, K), yh[1, j].reshape(ch, K)], axis=1)
        res = jnp.dot(pair, both, preferred_element_type=F32)
        basis_v[j] = (res[:, :K] + res[:, K:]).astype(BF16)
        c = pltpu.make_async_copy(
            basis_v.at[j], basis_hbm.at[pl.ds(pl.multiple_of(lax.rem(y + j, NY) * ch, ch), ch), :], out_sem.at[j]
        )
        c.start()
        outs.append(c)

    total = w2[z]
    for o in range(1, NZ):
        zz[o - 1].wait_recv()
        total = total + c3[o]
    scale = 1.0 / jnp.sqrt(jnp.float32(total_rows))
    coef_v[...] = jnp.dot(total, inverse_t, precision=HIGH, preferred_element_type=F32) * scale
    c = pltpu.make_async_copy(coef_v, coef_hbm, out_sem.at[NY])
    c.start()
    outs.append(c)
    for c in outs:
        c.wait()
    for c in sent:
        c.wait_send()


def body(panel, omega, order):
    rows, cols = panel.shape
    ch = rows // NY
    half = ch // 2
    total_rows = rows * lax.axis_size("rows")
    dma = pltpu.SemaphoreType.DMA
    vmem = pltpu.VMEM
    per = K // NG
    return pl.pallas_call(
        functools.partial(kernel, total_rows),
        out_shape=(jax.ShapeDtypeStruct((rows, K), BF16), jax.ShapeDtypeStruct((16, K), F32)),
        in_specs=[
            pl.BlockSpec(memory_space=pl.ANY),
            pl.BlockSpec(memory_space=pl.ANY),
            pl.BlockSpec(memory_space=pltpu.VMEM),
        ],
        out_specs=(pl.BlockSpec(memory_space=pl.ANY), pl.BlockSpec(memory_space=pl.ANY)),
        scratch_shapes=[
            vmem((NY, ch, cols), BF16),
            vmem((cols, K), BF16),
            vmem((NY, 2, half, K), F32),
            vmem((7, half, K), F32),
            vmem((7, half, K), F32),
            vmem((NG, per, K), F32),
            vmem((NG, per, K), F32),
            vmem((NY, per, K), F32),
            vmem((NZ, per, K), F32),
            vmem((NG, per, K), F32),
            vmem((2, NY, 2, half, K), BF16),
            vmem((K, cols), F32),
            vmem((2, NG // 2, NZ, 16, K), F32),
            vmem((NG // 2, NZ, 16, K), F32),
            vmem((NG // 2, NZ, 16, K), F32),
            vmem((NG // 2, NZ, 16, K), F32),
            vmem((NZ, 16, K), F32),
            vmem((NZ, 16, K), F32),
            vmem((NY, ch, K), BF16),
            vmem((16, K), F32),
            dma((NY,)),
            dma,
            dma((NY + 1,)),
            dma((2, 7)),
            dma((2, 7)),
            dma((4, 8)),
            dma((4, 8)),
            dma((2, 2, 8)),
            dma((2, 2, 8)),
            dma((12,)),
            dma((12,)),
        ],
        compiler_params=pltpu.CompilerParams(
            collective_id=0, has_side_effects=True, vmem_limit_bytes=48 * 1024 * 1024
        ),
        cost_estimate=pl.CostEstimate(flops=1_300_000_000, bytes_accessed=5_000_000, transcendentals=0),
    )(panel, omega, order.reshape(1, K))


def solution(mesh):
    in_specs = (P("rows", "cols"), P("cols", None), P())
    out_specs = (P("rows", None), P(("cols", "rows"), None))
    return jax.shard_map(body, mesh=mesh, in_specs=in_specs, out_specs=out_specs, check_vma=False)
```

```python
import functools

import jax
import jax.numpy as jnp
from jax import lax
from jax.experimental import pallas as pl
from jax.experimental.pallas import tpu as pltpu
from jax.sharding import PartitionSpec as P

F32 = jnp.float32
BF16 = jnp.bfloat16
MESH = pl.DeviceIdType.MESH
K = 128
NY = 8
NZ = 8
NG = 8
HIGH = lax.Precision.HIGHEST

CUTS = 2
RIGHTWARD = tuple(
    (j, h * CUTS + c) for j, h in ((4, 0), (3, 1), (3, 0), (2, 1), (2, 0), (1, 1), (1, 0)) for c in range(CUTS)
)
LEFTWARD = tuple(
    (j, h * CUTS + c) for j, h in ((4, 1), (5, 0), (5, 1), (6, 0), (6, 1), (7, 0), (7, 1)) for c in range(CUTS)
)
AHEAD = 2 * CUTS
CHUNKS = (4, 3, 5, 2, 6, 1, 7, 0)


def wide(v):
    return jnp.broadcast_to(v, (8, K))


def factor_block(rows, done, k):
    lane = lax.broadcasted_iota(jnp.int32, (8, K), 1)
    sub = lax.broadcasted_iota(jnp.int32, (8, K), 0)
    b0 = k // 8
    here = rows[b0]
    inside = (lane >= k) & (lane < k + 8)
    cols = [wide(here[:, k + j : k + j + 1]) for j in range(8)]
    s = {(i, j): cols[j][i : i + 1, :] for i in range(8) for j in range(i + 1)}
    mod = jnp.where(inside, jnp.where(lane - k == sub, 1.0, 0.0), here)
    b = [mod[i : i + 1, :] for i in range(8)]
    r, low = [], {}
    for j in range(8):
        r.append(pltpu.reciprocal(s[j, j], approx=False))
        for i in range(j + 1, 8):
            low[i, j] = s[i, j] * r[j]
        for i in range(j + 1, 8):
            for m in range(j + 1, i + 1):
                s[i, m] = s[i, m] - low[i, j] * s[m, j]
    for j in range(8):
        for i in range(j + 1, 8):
            b[i] = b[i] - low[i, j] * b[j]
    al = [b[j] * r[j] for j in range(8)]
    for j in reversed(range(8)):
        for m in range(j):
            al[m] = al[m] - low[j, m] * al[j]
    out = jnp.zeros((8, K), F32)
    for j in range(8):
        out = jnp.where(sub == j, wide(b[j] * lax.rsqrt(s[j, j])), out)
    done.append(jnp.where(lane <= sub + k, out, 0.0))
    al = [wide(v) for v in al]
    for i in range(b0 + 1, 16):
        t = [wide(rows[i][:, k + j : k + j + 1]) * al[j] for j in range(8)]
        while len(t) > 1:
            t = [t[n] + t[n + 1] for n in range(0, len(t), 2)]
        rows[i] = jnp.where(inside, 0.0, rows[i]) - t[0]


def kernel(
    total_rows, panel_hbm, omega_hbm, order_hbm, basis_ref, coef_ref,
    panel_v, omega_v, order_v, py, rr, rl, gram_v, a1, a2, a3, gram_f, yh, zt, zr, c1, w1, c2, w2, c3,
    panel_sem, omega_sem, order_sem, rs_send, rs_recv, g_send, g_recv, ag_send, ag_recv, z_send, z_recv,
    z_word, x_word,
):
    rows_at = lax.axis_index("rows")
    y = lax.axis_index("cols")
    z = rows_at // NG
    g = lax.rem(rows_at, NG)
    x = g // 2
    core = lax.rem(g, 2)
    nx = NG // 2

    def at_y(o):
        return (rows_at, lax.rem(y + o, NY))

    def at_z(o):
        return (lax.rem(z + o, NZ) * NG + g, y)

    def at_g(o):
        return (z * NG + lax.rem(g + o, NG), y)

    def send(src, dst, send_sem, recv_sem, device):
        c = pltpu.make_async_remote_copy(
            src_ref=src, dst_ref=dst, send_sem=send_sem, recv_sem=recv_sem, device_id=device, device_id_type=MESH
        )
        c.start()
        sent.append(c)
        return c

    sent = []
    ch = panel_v.shape[1]
    half = ch // 2

    barrier = pltpu.get_barrier_semaphore()
    beside_z = (at_z(1), at_z(NZ - 1))
    beside_x = tuple((z * NG + lax.rem(x + o, nx) * 2 + core, y) for o in (1, nx - 1))
    other = (z * NG + g + 1 - 2 * core, y)
    partners = (at_y(1), at_y(NY - 1)) + beside_z + beside_x + (other,)
    for device in partners:
        pl.semaphore_signal(barrier, inc=1, device_id=device, device_id_type=MESH)

    loads = {}
    om = pltpu.make_async_copy(omega_hbm, omega_v, omega_sem)
    om.start()
    od = pltpu.make_async_copy(order_hbm, order_v, order_sem)
    od.start()
    for j in CHUNKS:
        loads[j] = pltpu.make_async_copy(
            panel_hbm.at[pl.ds(pl.multiple_of(lax.rem(y + j, NY) * ch, ch), ch), :], panel_v.at[j], panel_sem.at[j]
        )
        loads[j].start()

    om.wait()
    od.wait()
    picker = (order_v[...] == lax.broadcasted_iota(jnp.int32, (K, K), 0)).astype(BF16)
    omega_v[...] = jnp.dot(omega_v[...], picker, preferred_element_type=F32).astype(BF16)

    def sketch(j):
        loads[j].wait()
        py[j] = jnp.dot(panel_v[j], omega_v[...], preferred_element_type=F32).reshape(2 * CUTS, half // CUTS, K)

    right, left = at_y(1), at_y(NY - 1)
    copies_r, copies_l = [], []

    def rs_right(i):
        j, h = RIGHTWARD[i]
        if i >= AHEAD:
            copies_r[i - AHEAD].wait_recv()
            py[j, h] = py[j, h] + rr[i - AHEAD]
        copies_r.append(send(py.at[j, h], rr.at[i], rs_send.at[0, i], rs_recv.at[0, i], right))

    def rs_left(i):
        j, h = LEFTWARD[i]
        if i >= AHEAD:
            copies_l[i - AHEAD].wait_recv()
            py[j, h] = py[j, h] + rl[i - AHEAD]
        copies_l.append(send(py.at[j, h], rl.at[i], rs_send.at[1, i], rs_recv.at[1, i], left))

    def relay(level):
        for sems, pair, levels in ((z_word, beside_z, 3), (x_word, beside_x, 2)):
            for way in (0, 1):
                if 0 < level <= levels:
                    pl.semaphore_wait(sems.at[level - 1, way], 1)
            for way in (0, 1):
                if level < levels:
                    pl.semaphore_signal(sems.at[level, way], inc=1, device_id=pair[way], device_id_type=MESH)

    sketch(4)
    pl.semaphore_wait(barrier, len(partners))
    for i in range(CUTS):
        rs_right(i)
        rs_left(i)
    sketch(3)
    for i in range(CUTS, AHEAD):
        rs_right(i)
    sketch(5)
    for i in range(CUTS, AHEAD):
        rs_left(i)
    relay(0)
    for j in (2, 6, 1, 7, 0):
        sketch(j)
    last = len(RIGHTWARD)
    for i in range(AHEAD, last):
        rs_right(i)
        rs_left(i)
        if i == AHEAD + 2:
            relay(1)
        if i == AHEAD + 5:
            relay(2)
        if i == AHEAD + 8:
            relay(3)
    parts = [py[0, q] for q in range(AHEAD)]
    for i in range(last - AHEAD, last):
        copies_r[i].wait_recv()
        q = RIGHTWARD[i][1]
        parts[q] = parts[q] + rr[i]
        copies_l[i].wait_recv()
        q = LEFTWARD[i][1]
        parts[q] = parts[q] + rl[i]
    share = jnp.concatenate(parts, axis=0)

    gram_v[...] = (
        lax.dot_general(share, share, (((0,), (0,)), ((), ())), precision=HIGH, preferred_element_type=F32) / total_rows
    ).reshape(NG, K // NG, K)
    st1 = [
        send(gram_v.at[lax.rem(g + o, NG)], a1.at[o], g_send.at[0, o], g_recv.at[0, o], at_g(o)) for o in range(1, NG)
    ]
    share_hi = share.astype(BF16)
    yh[0, 0] = share_hi.reshape(2, half, K)
    yh[1, 0] = (share - share_hi.astype(F32)).astype(BF16).reshape(2, half, K)

    hops = {}

    def gather_hop(kind, s):
        for h in (0, 1):
            for way, device in ((0, right), (1, left)):
                src = (NY - s) % NY if way == 0 else s
                dst = NY - 1 - s if way == 0 else s + 1
                if s > 0:
                    hops[kind, s - 1, way, h].wait_recv()
                if s < 3 or h == way:
                    i = 2 * s + h
                    hops[kind, s, way, h] = send(
                        yh.at[kind, src, h], yh.at[kind, dst, h], ag_send.at[kind, way, i], ag_recv.at[kind, way, i],
                        device,
                    )

    def finish_gather(kind):
        for way in (0, 1):
            hops[kind, 3, way, way].wait_recv()

    def project(j, first=False):
        term = lax.dot_general(
            yh[0, j].reshape(ch, K), panel_v[j], (((0,), (0,)), ((), ())), preferred_element_type=F32
        )
        zt[...] = term if first else zt[...] + term

    gather_hop(0, 0)
    project(0, True)
    for c in st1:
        c.wait_recv()
    part = gram_v[g]
    for o in range(1, NG):
        part = part + a1[o]
    a2[z] = part
    st2 = [send(a2.at[z], a2.at[z], g_send.at[1, o], g_recv.at[1, o], at_z(o)) for o in range(1, NZ)]

    gather_hop(0, 1)
    project(7)
    project(1)
    gather_hop(0, 2)
    project(6)
    project(2)
    for c in st2:
        c.wait_recv()
    part = a2[0]
    for o in range(1, NZ):
        part = part + a2[o]
    a3[y] = part
    st3 = [send(a3.at[y], a3.at[y], g_send.at[2, o], g_recv.at[2, o], at_y(o)) for o in range(1, NY)]

    gather_hop(0, 3)
    gather_hop(1, 0)
    project(5)
    project(3)
    for c in st3:
        c.wait_recv()
    part = a3[0]
    for o in range(1, NY):
        part = part + a3[o]
    gram_f[g] = part
    st4 = [send(gram_f.at[g], gram_f.at[g], g_send.at[3, o], g_recv.at[3, o], at_g(o)) for o in range(1, NG)]

    finish_gather(0)
    project(4)
    per_z = NG * 16
    for b in range(NZ):
        block = zt[:, b * per_z : (b + 1) * per_z].T.reshape(nx, 2, 16, K)
        for h in range(2):
            for i in range(nx):
                zr[h, i, b] = block[i, h]
    zc = send(zr.at[1 - core], c1, z_send.at[0], z_recv.at[0], other)
    gather_hop(1, 1)
    zc.wait_recv()
    w1[...] = zr[core] + c1[...]
    zx = [
        send(
            w1.at[lax.rem(x + o, nx)], c2.at[o], z_send.at[o], z_recv.at[o],
            (z * NG + lax.rem(x + o, nx) * 2 + core, y),
        )
        for o in range(1, nx)
    ]
    for c in st4:
        c.wait_recv()
    matrix = gram_f[...].reshape(K, K)
    blocks = [matrix[8 * i : 8 * i + 8, :] for i in range(16)]
    done = []
    for k in range(0, 16, 8):
        factor_block(blocks, done, k)
    gather_hop(1, 2)
    for k in range(16, 40, 8):
        factor_block(blocks, done, k)
    total = w1[x]
    for o in range(1, nx):
        zx[o - 1].wait_recv()
        total = total + c2[o]
    w2[...] = total
    zz = [
        send(w2.at[lax.rem(z + o, NZ)], c3.at[o], z_send.at[3 + o], z_recv.at[3 + o], at_z(o)) for o in range(1, NZ)
    ]
    for k in range(40, 72, 8):
        factor_block(blocks, done, k)
    gather_hop(1, 3)
    for k in range(72, 128, 8):
        factor_block(blocks, done, k)

    inverse_t = jnp.concatenate(done, axis=0).T
    inv_hi = inverse_t.astype(BF16)
    inv_lo = (inverse_t - inv_hi.astype(F32)).astype(BF16)
    both = jnp.concatenate([inv_hi, inv_lo], axis=1)
    both = jnp.concatenate([both, both], axis=0)
    finish_gather(1)
    for j in range(NY):
        pair = jnp.concatenate([yh[0, j].reshape(ch, K), yh[1, j].reshape(ch, K)], axis=1)
        res = jnp.dot(pair, both, preferred_element_type=F32)
        basis_ref[pl.ds(pl.multiple_of(lax.rem(y + j, NY) * ch, ch), ch), :] = (res[:, :K] + res[:, K:]).astype(BF16)

    total = w2[z]
    for o in range(1, NZ):
        zz[o - 1].wait_recv()
        total = total + c3[o]
    scale = 1.0 / jnp.sqrt(jnp.float32(total_rows))
    coef_ref[...] = jnp.dot(total, inverse_t, precision=HIGH, preferred_element_type=F32) * scale
    for c in sent:
        c.wait_send()


def body(panel, omega, order):
    rows, cols = panel.shape
    ch = rows // NY
    half = ch // 2
    total_rows = rows * lax.axis_size("rows")
    dma = pltpu.SemaphoreType.DMA
    vmem = pltpu.VMEM
    per = K // NG
    return pl.pallas_call(
        functools.partial(kernel, total_rows),
        out_shape=(jax.ShapeDtypeStruct((rows, K), BF16), jax.ShapeDtypeStruct((16, K), F32)),
        in_specs=[
            pl.BlockSpec(memory_space=pltpu.HBM),
            pl.BlockSpec(memory_space=pltpu.HBM),
            pl.BlockSpec(memory_space=pltpu.HBM),
        ],
        out_specs=(pl.BlockSpec(memory_space=vmem), pl.BlockSpec(memory_space=vmem)),
        scratch_shapes=[
            vmem((NY, ch, cols), BF16),
            vmem((cols, K), BF16),
            vmem((1, K), jnp.int32),
            vmem((NY, 2 * CUTS, half // CUTS, K), F32),
            vmem((7 * CUTS, half // CUTS, K), F32),
            vmem((7 * CUTS, half // CUTS, K), F32),
            vmem((NG, per, K), F32),
            vmem((NG, per, K), F32),
            vmem((NY, per, K), F32),
            vmem((NZ, per, K), F32),
            vmem((NG, per, K), F32),
            vmem((2, NY, 2, half, K), BF16),
            vmem((K, cols), F32),
            vmem((2, NG // 2, NZ, 16, K), F32),
            vmem((NG // 2, NZ, 16, K), F32),
            vmem((NG // 2, NZ, 16, K), F32),
            vmem((NG // 2, NZ, 16, K), F32),
            vmem((NZ, 16, K), F32),
            vmem((NZ, 16, K), F32),
            dma((NY,)),
            dma,
            dma,
            dma((2, 7 * CUTS)),
            dma((2, 7 * CUTS)),
            dma((4, 8)),
            dma((4, 8)),
            dma((2, 2, 8)),
            dma((2, 2, 8)),
            dma((12,)),
            dma((12,)),
            pltpu.SemaphoreType.REGULAR((3, 2)),
            pltpu.SemaphoreType.REGULAR((2, 2)),
        ],
        compiler_params=pltpu.CompilerParams(
            collective_id=0, has_side_effects=True, vmem_limit_bytes=48 * 1024 * 1024
        ),
        cost_estimate=pl.CostEstimate(flops=1_300_000_000, bytes_accessed=5_000_000, transcendentals=0),
    )(
        pltpu.with_memory_space_constraint(panel, pltpu.HBM),
        pltpu.with_memory_space_constraint(omega, pltpu.HBM),
        pltpu.with_memory_space_constraint(order.reshape(1, K), pltpu.HBM),
    )


def solution(mesh):
    in_specs = (P("rows", "cols"), P("cols", None), P())
    out_specs = (P("rows", None), P(("cols", "rows"), None))
    return jax.shard_map(body, mesh=mesh, in_specs=in_specs, out_specs=out_specs, check_vma=False)
```

```python
import functools

import jax
import jax.numpy as jnp
from jax import lax
from jax.experimental import pallas as pl
from jax.experimental.pallas import tpu as pltpu
from jax.sharding import PartitionSpec as P

F32 = jnp.float32
BF16 = jnp.bfloat16
MESH = pl.DeviceIdType.MESH
K = 128
NY = 8
NZ = 8
NG = 8
HIGH = lax.Precision.HIGHEST

CUTS = 2
RIGHTWARD = tuple(
    (j, h * CUTS + c) for j, h in ((4, 0), (3, 1), (3, 0), (2, 1), (2, 0), (1, 1), (1, 0)) for c in range(CUTS)
)
LEFTWARD = tuple(
    (j, h * CUTS + c) for j, h in ((4, 1), (5, 0), (5, 1), (6, 0), (6, 1), (7, 0), (7, 1)) for c in range(CUTS)
)
AHEAD = 2 * CUTS
CHUNKS = (4, 3, 5, 2, 6, 1, 7, 0)


def wide(v):
    return jnp.broadcast_to(v, (8, K))


def factor_block(rows, done, k):
    lane = lax.broadcasted_iota(jnp.int32, (8, K), 1)
    sub = lax.broadcasted_iota(jnp.int32, (8, K), 0)
    b0 = k // 8
    here = rows[b0]
    inside = (lane >= k) & (lane < k + 8)
    cols = [wide(here[:, k + j : k + j + 1]) for j in range(8)]
    s = {(i, j): cols[j][i : i + 1, :] for i in range(8) for j in range(i + 1)}
    mod = jnp.where(inside, jnp.where(lane - k == sub, 1.0, 0.0), here)
    b = [mod[i : i + 1, :] for i in range(8)]
    r, low = [], {}
    for j in range(8):
        r.append(pltpu.reciprocal(s[j, j], approx=False))
        for i in range(j + 1, 8):
            low[i, j] = s[i, j] * r[j]
        for i in range(j + 1, 8):
            for m in range(j + 1, i + 1):
                s[i, m] = s[i, m] - low[i, j] * s[m, j]
    for j in range(8):
        for i in range(j + 1, 8):
            b[i] = b[i] - low[i, j] * b[j]
    al = [b[j] * r[j] for j in range(8)]
    for j in reversed(range(8)):
        for m in range(j):
            al[m] = al[m] - low[j, m] * al[j]
    out = jnp.zeros((8, K), F32)
    for j in range(8):
        out = jnp.where(sub == j, wide(b[j] * lax.rsqrt(s[j, j])), out)
    done.append(jnp.where(lane <= sub + k, out, 0.0))
    al = [wide(v) for v in al]
    for i in range(b0 + 1, 16):
        t = [wide(rows[i][:, k + j : k + j + 1]) * al[j] for j in range(8)]
        while len(t) > 1:
            t = [t[n] + t[n + 1] for n in range(0, len(t), 2)]
        rows[i] = jnp.where(inside, 0.0, rows[i]) - t[0]


def kernel(
    total_rows, panel_hbm, omega_hbm, order_hbm, basis_ref, coef_ref,
    panel_v, omega_v, order_v, py, rr, rl, gram_v, a1, a2, a3, gram_f, yh, zt, zr, c1, w1, c2, w2, c3,
    panel_sem, omega_sem, order_sem, rs_send, rs_recv, g_send, g_recv, ag_send, ag_recv, z_send, z_recv,
    z_word, x_word,
):
    rows_at = lax.axis_index("rows")
    y = lax.axis_index("cols")
    z = rows_at // NG
    g = lax.rem(rows_at, NG)
    x = g // 2
    core = lax.rem(g, 2)
    nx = NG // 2

    def at_y(o):
        return (rows_at, lax.rem(y + o, NY))

    def at_z(o):
        return (lax.rem(z + o, NZ) * NG + g, y)

    def at_g(o):
        return (z * NG + lax.rem(g + o, NG), y)

    def send(src, dst, send_sem, recv_sem, device):
        c = pltpu.make_async_remote_copy(
            src_ref=src, dst_ref=dst, send_sem=send_sem, recv_sem=recv_sem, device_id=device, device_id_type=MESH
        )
        c.start()
        sent.append(c)
        return c

    sent = []
    ch = panel_v.shape[1]
    half = ch // 2

    barrier = pltpu.get_barrier_semaphore()
    beside_z = (at_z(1), at_z(NZ - 1))
    beside_x = tuple((z * NG + lax.rem(x + o, nx) * 2 + core, y) for o in (1, nx - 1))
    other = (z * NG + g + 1 - 2 * core, y)
    partners = (at_y(1), at_y(NY - 1)) + beside_z + beside_x + (other,)
    for device in partners:
        pl.semaphore_signal(barrier, inc=1, device_id=device, device_id_type=MESH)

    loads = {}
    om = pltpu.make_async_copy(omega_hbm, omega_v, omega_sem)
    om.start()
    od = pltpu.make_async_copy(order_hbm, order_v, order_sem)
    od.start()
    for j in CHUNKS:
        loads[j] = pltpu.make_async_copy(
            panel_hbm.at[pl.ds(pl.multiple_of(lax.rem(y + j, NY) * ch, ch), ch), :], panel_v.at[j], panel_sem.at[j]
        )
        loads[j].start()

    om.wait()
    od.wait()
    picker = (order_v[...] == lax.broadcasted_iota(jnp.int32, (K, K), 0)).astype(BF16)
    omega_v[...] = jnp.dot(omega_v[...], picker, preferred_element_type=F32).astype(BF16)

    def sketch(j):
        loads[j].wait()
        py[j] = jnp.dot(panel_v[j], omega_v[...], preferred_element_type=F32).reshape(2 * CUTS, half // CUTS, K)

    right, left = at_y(1), at_y(NY - 1)
    copies_r, copies_l = [], []

    def rs_right(i):
        j, h = RIGHTWARD[i]
        if i >= AHEAD:
            copies_r[i - AHEAD].wait_recv()
            py[j, h] = py[j, h] + rr[i - AHEAD]
        copies_r.append(send(py.at[j, h], rr.at[i], rs_send.at[0, i], rs_recv.at[0, i], right))

    def rs_left(i):
        j, h = LEFTWARD[i]
        if i >= AHEAD:
            copies_l[i - AHEAD].wait_recv()
            py[j, h] = py[j, h] + rl[i - AHEAD]
        copies_l.append(send(py.at[j, h], rl.at[i], rs_send.at[1, i], rs_recv.at[1, i], left))

    def relay(level):
        for sems, pair, levels in ((z_word, beside_z, 3), (x_word, beside_x, 2)):
            for way in (0, 1):
                if 0 < level <= levels:
                    pl.semaphore_wait(sems.at[level - 1, way], 1)
            for way in (0, 1):
                if level < levels:
                    pl.semaphore_signal(sems.at[level, way], inc=1, device_id=pair[way], device_id_type=MESH)

    sketch(4)
    pl.semaphore_wait(barrier, len(partners))
    for i in range(CUTS):
        rs_right(i)
        rs_left(i)
    sketch(3)
    for i in range(CUTS, AHEAD):
        rs_right(i)
    sketch(5)
    for i in range(CUTS, AHEAD):
        rs_left(i)
    relay(0)
    for j in (2, 6, 1, 7, 0):
        sketch(j)
    last = len(RIGHTWARD)
    for i in range(AHEAD, last):
        rs_right(i)
        rs_left(i)
        if i == AHEAD + 2:
            relay(1)
        if i == AHEAD + 5:
            relay(2)
        if i == AHEAD + 8:
            relay(3)
    parts = [py[0, q] for q in range(AHEAD)]
    for i in range(last - AHEAD, last):
        copies_r[i].wait_recv()
        q = RIGHTWARD[i][1]
        parts[q] = parts[q] + rr[i]
        copies_l[i].wait_recv()
        q = LEFTWARD[i][1]
        parts[q] = parts[q] + rl[i]
    share = jnp.concatenate(parts, axis=0)

    gram_v[...] = (
        lax.dot_general(share, share, (((0,), (0,)), ((), ())), precision=HIGH, preferred_element_type=F32) / total_rows
    ).reshape(NG, K // NG, K)
    st1 = [
        send(gram_v.at[lax.rem(g + o, NG)], a1.at[o], g_send.at[0, o], g_recv.at[0, o], at_g(o)) for o in range(1, NG)
    ]
    share_hi = share.astype(BF16)
    yh[0, 0] = share_hi.reshape(2, half, K)
    yh[1, 0] = (share - share_hi.astype(F32)).astype(BF16).reshape(2, half, K)

    hops = {}

    def gather_hop(kind, s):
        if kind == 1 and s < 3:
            for way, device in ((0, right), (1, left)):
                src = (NY - s) % NY if way == 0 else s
                dst = NY - 1 - s if way == 0 else s + 1
                if s > 0:
                    hops[kind, s - 1, way, 0].wait_recv()
                hops[kind, s, way, 0] = send(
                    yh.at[kind, src], yh.at[kind, dst], ag_send.at[kind, way, s], ag_recv.at[kind, way, s], device
                )
            return
        if kind == 1:
            for way, device in ((0, right), (1, left)):
                hops[kind, 2, way, 0].wait_recv()
                src = (NY - s) % NY if way == 0 else s
                hops[kind, s, way, way] = send(
                    yh.at[kind, src, way], yh.at[kind, 4, way], ag_send.at[kind, way, s], ag_recv.at[kind, way, s], device
                )
            return
        for h in (0, 1):
            for way, device in ((0, right), (1, left)):
                src = (NY - s) % NY if way == 0 else s
                dst = NY - 1 - s if way == 0 else s + 1
                if s > 0:
                    hops[kind, s - 1, way, h].wait_recv()
                if s < 3 or h == way:
                    i = 2 * s + h
                    hops[kind, s, way, h] = send(
                        yh.at[kind, src, h], yh.at[kind, dst, h], ag_send.at[kind, way, i], ag_recv.at[kind, way, i],
                        device,
                    )

    def finish_gather(kind):
        for way in (0, 1):
            hops[kind, 3, way, way].wait_recv()

    def project(j, first=False):
        term = lax.dot_general(
            yh[0, j].reshape(ch, K), panel_v[j], (((0,), (0,)), ((), ())), preferred_element_type=F32
        )
        zt[...] = term if first else zt[...] + term

    gather_hop(0, 0)
    project(0, True)
    for c in st1:
        c.wait_recv()
    part = gram_v[g]
    for o in range(1, NG):
        part = part + a1[o]
    a2[z] = part
    st2 = [send(a2.at[z], a2.at[z], g_send.at[1, o], g_recv.at[1, o], at_z(o)) for o in range(1, NZ)]

    gather_hop(0, 1)
    project(7)
    project(1)
    gather_hop(0, 2)
    project(6)
    project(2)
    for c in st2:
        c.wait_recv()
    part = a2[0]
    for o in range(1, NZ):
        part = part + a2[o]
    a3[y] = part
    st3 = [send(a3.at[y], a3.at[y], g_send.at[2, o], g_recv.at[2, o], at_y(o)) for o in range(1, NY)]

    gather_hop(0, 3)
    gather_hop(1, 0)
    project(5)
    project(3)
    for c in st3:
        c.wait_recv()
    part = a3[0]
    for o in range(1, NY):
        part = part + a3[o]
    gram_f[g] = part
    st4 = [send(gram_f.at[g], gram_f.at[g], g_send.at[3, o], g_recv.at[3, o], at_g(o)) for o in range(1, NG)]

    finish_gather(0)
    project(4)
    per_z = NG * 16
    for b in range(NZ):
        block = zt[:, b * per_z : (b + 1) * per_z].T.reshape(nx, 2, 16, K)
        for h in range(2):
            for i in range(nx):
                zr[h, i, b] = block[i, h]
    zc = send(zr.at[1 - core], c1, z_send.at[0], z_recv.at[0], other)
    gather_hop(1, 1)
    zc.wait_recv()
    w1[...] = zr[core] + c1[...]
    zx = [
        send(
            w1.at[lax.rem(x + o, nx)], c2.at[o], z_send.at[o], z_recv.at[o],
            (z * NG + lax.rem(x + o, nx) * 2 + core, y),
        )
        for o in range(1, nx)
    ]
    for c in st4:
        c.wait_recv()
    matrix = gram_f[...].reshape(K, K)
    blocks = [matrix[8 * i : 8 * i + 8, :] for i in range(16)]
    done = []
    for k in range(0, 16, 8):
        factor_block(blocks, done, k)
    gather_hop(1, 2)
    for k in range(16, 40, 8):
        factor_block(blocks, done, k)
    total = w1[x]
    for o in range(1, nx):
        zx[o - 1].wait_recv()
        total = total + c2[o]
    w2[...] = total
    zz = [
        send(w2.at[lax.rem(z + o, NZ)], c3.at[o], z_send.at[3 + o], z_recv.at[3 + o], at_z(o)) for o in range(1, NZ)
    ]
    for k in range(40, 72, 8):
        factor_block(blocks, done, k)
    gather_hop(1, 3)
    for k in range(72, 128, 8):
        factor_block(blocks, done, k)

    inverse_t = jnp.concatenate(done, axis=0).T
    inv_hi = inverse_t.astype(BF16)
    inv_lo = (inverse_t - inv_hi.astype(F32)).astype(BF16)
    both = jnp.concatenate([inv_hi, inv_lo], axis=1)
    both = jnp.concatenate([both, both], axis=0)
    finish_gather(1)
    for j in range(NY):
        pair = jnp.concatenate([yh[0, j].reshape(ch, K), yh[1, j].reshape(ch, K)], axis=1)
        res = jnp.dot(pair, both, preferred_element_type=F32)
        basis_ref[pl.ds(pl.multiple_of(lax.rem(y + j, NY) * ch, ch), ch), :] = (res[:, :K] + res[:, K:]).astype(BF16)

    total = w2[z]
    for o in range(1, NZ):
        zz[o - 1].wait_recv()
        total = total + c3[o]
    scale = 1.0 / jnp.sqrt(jnp.float32(total_rows))
    coef_ref[...] = jnp.dot(total, inverse_t, precision=HIGH, preferred_element_type=F32) * scale
    for c in sent:
        c.wait_send()


def body(panel, omega, order):
    rows, cols = panel.shape
    ch = rows // NY
    half = ch // 2
    total_rows = rows * lax.axis_size("rows")
    dma = pltpu.SemaphoreType.DMA
    vmem = pltpu.VMEM
    per = K // NG
    return pl.pallas_call(
        functools.partial(kernel, total_rows),
        out_shape=(jax.ShapeDtypeStruct((rows, K), BF16), jax.ShapeDtypeStruct((16, K), F32)),
        in_specs=[
            pl.BlockSpec(memory_space=pltpu.HBM),
            pl.BlockSpec(memory_space=pltpu.HBM),
            pl.BlockSpec(memory_space=pltpu.HBM),
        ],
        out_specs=(pl.BlockSpec(memory_space=vmem), pl.BlockSpec(memory_space=vmem)),
        scratch_shapes=[
            vmem((NY, ch, cols), BF16),
            vmem((cols, K), BF16),
            vmem((1, K), jnp.int32),
            vmem((NY, 2 * CUTS, half // CUTS, K), F32),
            vmem((7 * CUTS, half // CUTS, K), F32),
            vmem((7 * CUTS, half // CUTS, K), F32),
            vmem((NG, per, K), F32),
            vmem((NG, per, K), F32),
            vmem((NY, per, K), F32),
            vmem((NZ, per, K), F32),
            vmem((NG, per, K), F32),
            vmem((2, NY, 2, half, K), BF16),
            vmem((K, cols), F32),
            vmem((2, NG // 2, NZ, 16, K), F32),
            vmem((NG // 2, NZ, 16, K), F32),
            vmem((NG // 2, NZ, 16, K), F32),
            vmem((NG // 2, NZ, 16, K), F32),
            vmem((NZ, 16, K), F32),
            vmem((NZ, 16, K), F32),
            dma((NY,)),
            dma,
            dma,
            dma((2, 7 * CUTS)),
            dma((2, 7 * CUTS)),
            dma((4, 8)),
            dma((4, 8)),
            dma((2, 2, 8)),
            dma((2, 2, 8)),
            dma((12,)),
            dma((12,)),
            pltpu.SemaphoreType.REGULAR((3, 2)),
            pltpu.SemaphoreType.REGULAR((2, 2)),
        ],
        compiler_params=pltpu.CompilerParams(
            collective_id=0, has_side_effects=True, vmem_limit_bytes=48 * 1024 * 1024
        ),
        cost_estimate=pl.CostEstimate(flops=1_300_000_000, bytes_accessed=5_000_000, transcendentals=0),
    )(
        pltpu.with_memory_space_constraint(panel, pltpu.HBM),
        pltpu.with_memory_space_constraint(omega, pltpu.HBM),
        pltpu.with_memory_space_constraint(order.reshape(1, K), pltpu.HBM),
    )


def solution(mesh):
    in_specs = (P("rows", "cols"), P("cols", None), P())
    out_specs = (P("rows", None), P(("cols", "rows"), None))
    return jax.shard_map(body, mesh=mesh, in_specs=in_specs, out_specs=out_specs, check_vma=False)
```
